32 devices in a mesh: row: 8 (over y, x, core), col: 4 (over z).
Axes of the slice: x: 2, y: 2, z: 4, core: 2. Of those that a mesh axis runs over, the one named last changes fastest.
Arguments:
- kernel: float32 [6, 4096, 2, 2048], P(None, 'row', None, 'col'), may hold values from 0 to 1, as said below
- jitter: float32 [2, 2048], P(None, 'col'), may hold values from 0.05 to 0.5
Outputs:
- factored: float32 [6, 4096, 2, 2048], P(None, 'row', None, 'col')
The draws below stay inside these ranges and needn't reach their ends.
Inputs may be any that keep to these rules, and one draw needn't show every extreme that they name: kernel is the matrix of a positive definite kernel function evaluated at 24576 demonstration states (rows) and the first 4096 of them (columns); it equals 1 on the diagonal.
All inputs are finite; a program needn't handle non-finite values.
Results may differ from the reference program's by a relative error of at most 0.0003.
Values sent between devices are 32-bit elements; how exact they have to be, the bound alone decides.
A program may use at most 192 MiB of HBM per device.

```python
import math
import jax
import jax.numpy as jnp
from jax import lax

NB = 512
RCYC = 6
CCYC = 2
ROWS = 24576
COLS = 4096
N_COL = 4


def draw_kernel(key, part):
    key = jax.random.fold_in(key, 7)
    phase_key, freq_key, offset_key, noise_key, weight_key = jax.random.split(key, 5)
    state_dims = 32
    phase = jax.random.uniform(phase_key, (ROWS, 1), jnp.float32)
    freq = jax.random.uniform(freq_key, (1, state_dims), jnp.float32, 1.0, 3.0)
    offset = jax.random.uniform(offset_key, (1, state_dims), jnp.float32, -math.pi, math.pi)
    weights = jax.random.uniform(weight_key, (state_dims,), jnp.float32, 0.5, 1.5) / 24.0
    path = jnp.sin(2.0 * math.pi * phase * freq + offset)
    states = path + 0.25 * jax.random.normal(noise_key, (ROWS, state_dims), jnp.float32)
    row_states = states.reshape(RCYC, ROWS // RCYC, state_dims)
    col_states = states[:COLS].reshape(CCYC, COLS // CCYC, state_dims)
    spread = jnp.zeros((RCYC, ROWS // RCYC, CCYC, COLS // CCYC), jnp.float32)
    for dim in range(state_dims):
        diff = row_states[:, :, None, None, dim] - col_states[None, None, :, :, dim]
        spread = spread + weights[dim] * jnp.abs(diff)
    return jnp.exp(-spread)


def block_levels(key, dims, cuts, smallest, top_value):
    level = 1.0
    for dim, blocks in cuts:
        steps = jax.random.uniform(jax.random.fold_in(jax.random.fold_in(key, 6), dim), (blocks,), jnp.float32, smallest / len(cuts), top_value / len(cuts))
        level = level * jnp.repeat(jnp.exp(steps), dims[dim] // blocks).reshape((-1,) + (1,) * (len(dims) - 1 - dim))
    return level


def setup_inputs(seed: int = 0) -> dict:
    seeds = jax.random.split(jax.random.key(seed), 3)
    kernel = draw_kernel(jax.random.fold_in(seeds[2], 71), 0)
    jitter = jnp.clip(jnp.exp(math.log(0.5) - 2.3025851 * jax.random.uniform(seeds[1], (CCYC, N_COL * NB), jnp.float32) ** block_levels(seeds[1], (CCYC, N_COL * NB), ((1, 4),), -0.2, 0.2)), 0.05, 0.5)
    return dict(kernel=kernel, jitter=jitter)


def reference(kernel, jitter):
    total_rows = kernel.shape[0] * kernel.shape[1]
    total_cols = kernel.shape[2] * kernel.shape[3]
    whole = kernel.reshape(total_rows, total_cols)
    diag_add = jitter.reshape(total_cols)
    row_ids = lax.broadcasted_iota(jnp.int32, (total_rows, total_cols), 0)
    col_ids = lax.broadcasted_iota(jnp.int32, (total_rows, total_cols), 1)
    lower = jnp.where(row_ids >= col_ids, whole, 0.0)
    lower = lower + jnp.where(row_ids == col_ids, diag_add[None, :], 0.0)
    for section in range(2):
        start = section * NB
        finish = (section + 1) * NB
        square = lower[start:finish, start:finish]
        sym = jnp.tril(square) + jnp.tril(square, -1).T
        factor = jnp.linalg.cholesky(sym)
        solved = lax.linalg.triangular_solve(factor, lower[:, start:finish], left_side=False, lower=True, transpose_a=True)
        panel = jnp.concatenate([jnp.zeros((start, NB), lower.dtype), factor, solved[finish:]], axis=0)
        update = jnp.dot(panel, panel[finish:total_cols].T, precision=lax.Precision.HIGHEST)
        lower = jnp.concatenate([lower[:, :start], panel, lower[:, finish:] - update], axis=1)
    result = jnp.where(row_ids >= col_ids, lower, 0.0)
    return result.reshape(kernel.shape)
```

```python
import functools

import jax
import jax.numpy as jnp
from jax import lax
from jax.experimental import pallas as pl
from jax.experimental.pallas import tpu as pltpu
from jax.sharding import PartitionSpec as P

BLOCK = 128
SUB = 8


def eliminate(square):
    groups = BLOCK // SUB
    rows = lax.broadcasted_iota(jnp.int32, (SUB, BLOCK), 0)
    lanes = lax.broadcasted_iota(jnp.int32, (SUB, BLOCK), 1)
    left = [square[g * SUB : (g + 1) * SUB, :] for g in range(groups)]
    right = [jnp.where(lanes == rows + g * SUB, 1.0, 0.0).astype(jnp.float32) for g in range(groups)]
    for k in range(BLOCK):
        home, inner = divmod(k, SUB)
        pivot = 1.0 / left[home][inner : inner + 1, k : k + 1]
        row_left = left[home][inner : inner + 1, :] * pivot
        row_right = right[home][inner : inner + 1, :] * pivot
        for g in range(home, groups):
            column = left[g][:, k : k + 1]
            if g == home:
                column = jnp.where(rows[:, :1] > inner, column, 0.0)
            left[g] = left[g] - column * row_left
            right[g] = right[g] - column * row_right
    done = []
    for g in range(groups):
        diagonal = jnp.sum(
            jnp.where(lanes == rows + g * SUB, left[g], 0.0), axis=1, keepdims=True
        )
        done.append(right[g] / jnp.sqrt(diagonal))
    return jnp.concatenate(done, axis=0)


def factor_kernel(lead_ref, inverse_ref, work_ref):
    size = lead_ref.shape[0]
    count = size // BLOCK
    width = size + BLOCK

    def start(i, carry):
        here = pl.ds(pl.multiple_of(i * BLOCK, BLOCK), BLOCK)
        work_ref[here, :size] = lead_ref[here, :]
        row = lax.broadcasted_iota(jnp.int32, (BLOCK, size), 0) + i * BLOCK
        lane = lax.broadcasted_iota(jnp.int32, (BLOCK, size), 1)
        work_ref[here, size:] = jnp.where(row == lane, 1.0, 0.0).astype(jnp.float32)
        return carry

    lax.fori_loop(0, count, start, 0)

    def step(k, carry):
        offset = pl.multiple_of(k * BLOCK, BLOCK)
        here = pl.ds(offset, BLOCK)
        window = pl.ds(offset, width)
        inverse = eliminate(work_ref[here, here])
        panel = jnp.dot(
            inverse, work_ref[here, window],
            precision=lax.Precision.HIGHEST, preferred_element_type=jnp.float32,
        )
        work_ref[here, window] = panel

        def reduce(i, carry):
            there = pl.ds(pl.multiple_of(i * BLOCK, BLOCK), BLOCK)
            product = lax.dot_general(
                work_ref[here, there], work_ref[here, window], (((0,), (0,)), ((), ())),
                precision=lax.Precision.HIGHEST, preferred_element_type=jnp.float32,
            )
            work_ref[there, window] = work_ref[there, window] - product
            return carry

        lax.fori_loop(k + 1, count, reduce, 0)
        return carry

    lax.fori_loop(0, count, step, 0)
    inverse_ref[...] = work_ref[:, size:]


def inverse_factor(lead):
    size = lead.shape[0]
    return pl.pallas_call(
        factor_kernel,
        out_shape=jax.ShapeDtypeStruct((size, size), jnp.float32),
        in_specs=[pl.BlockSpec(memory_space=pltpu.VMEM)],
        out_specs=pl.BlockSpec(memory_space=pltpu.VMEM),
        scratch_shapes=[pltpu.VMEM((size, 2 * size), jnp.float32)],
        compiler_params=pltpu.CompilerParams(vmem_limit_bytes=40 * 2**20),
        cost_estimate=pl.CostEstimate(
            flops=100_000_000_000, bytes_accessed=8 * size * size, transcendentals=0
        ),
        name="inverse_factor",
    )(lead)


DELAY = 2


def relay(own, col_count, col_index, before_step, first_free):
    cycles = len(own)
    order = [(1, 0), (1, 1)] if cycles > 1 else [(1, 0)]
    sent = [0, len(order)]
    while len(order) < 2 * cycles:
        turn = 0 if sent[0] < cycles and (order[-1][0] == 1 or sent[1] == cycles) else 1
        if turn == 0 and len(order) <= sent[0]:
            turn = 1
        order.append((turn, sent[turn]))
        sent[turn] += 1
    when = {item: step for step, item in enumerate(order)}
    steps = len(order) + DELAY * (col_count - 3)
    back = [lax.ppermute(own[a], "col", [(1, 0)]) for a in range(cycles)]
    got = []
    for step in range(steps):
        pairs = []
        value = None
        if step < cycles:
            value = own[step]
            pairs.append((0, 1))
        if step < len(order):
            panel, a = order[step]
            mine = own[a] if panel == 1 else got[a]
            value = mine if value is None else jnp.where(col_index == 1, mine, value)
            if col_count > 2:
                pairs.append((1, 2))
        passing = [c for c in range(2, col_count - 1) if 0 <= step - DELAY * (c - 1) < len(order)]
        if passing:
            before = got[step - DELAY]
            value = before if value is None else jnp.where(col_index >= 2, before, value)
            pairs.extend((c, c + 1) for c in passing)
        if step == first_free:
            value, _ = lax.optimization_barrier((value, before_step))
        got.append(lax.ppermute(value, "col", pairs))

    def found(panel, a):
        choices = [own[a] if panel == 0 else back[a], got[a] if panel == 0 else own[a]]
        choices += [got[when[panel, a] + DELAY * (c - 2)] for c in range(2, col_count)]
        value = choices[-1]
        for c in range(col_count - 2, -1, -1):
            value = jnp.where(col_index == c, choices[c], value)
        return value

    return [jnp.concatenate([found(0, a), found(1, a)], axis=1) for a in range(cycles)]


def times_transposed(left, right, precision):
    return lax.dot_general(
        left, right, (((1,), (1,)), ((), ())),
        precision=precision, preferred_element_type=jnp.float32,
    )


def body(kernel, jitter):
    row_cycles, tile, col_cycles, _ = kernel.shape
    row_count = lax.axis_size("row")
    col_count = lax.axis_size("col")
    row_index = lax.axis_index("row")
    col_index = lax.axis_index("col")
    rows = lax.broadcasted_iota(jnp.int32, (tile, tile), 0)
    cols = lax.broadcasted_iota(jnp.int32, (tile, tile), 1)
    slices = [kernel[:, :, cycle, :] for cycle in range(col_cycles)]

    def jittered(value, cycle, row_tile, col_tile):
        on = (rows == cols) & (row_tile == col_tile)
        return value + jnp.where(on, jitter[cycle][None, :], 0.0)

    def symmetric(square):
        return jnp.tril(square) + jnp.tril(square, -1).T

    corner = jittered(slices[0][0], 0, row_index, col_index)
    places = ((0, 0), (1, 0), (1, 1))
    kept = jnp.stack(
        [jnp.where((row_index == i) & (col_index == j), corner, 0.0) for i, j in places]
    )
    corner_sum = lax.psum(kept, ("row", "col"))
    first, below, second = corner_sum
    first, second = symmetric(first), symmetric(second)
    lead = jnp.concatenate(
        [jnp.concatenate([first, below.T], axis=1), jnp.concatenate([below, second], axis=1)], axis=0
    )
    inverse = inverse_factor(lead)

    raw = relay([slices[0][a] for a in range(row_cycles)], col_count, col_index, corner_sum, 2)

    wanted = [cycle * col_count + col_index for cycle in range(col_cycles)]
    kept = []
    for cycle in range(col_cycles):
        source = raw[0]
        for a in range(1, -(-(cycle + 1) * col_count // row_count)):
            source = jnp.where(wanted[cycle] // row_count == a, raw[a], source)
        kept.append(jnp.where(wanted[cycle] % row_count == row_index, source, 0.0))
    across = lax.psum(jnp.concatenate(kept, axis=0), "row")
    across = times_transposed(across, inverse, lax.Precision.HIGHEST)

    outs = []
    for a in range(row_cycles):
        row_tile = a * row_count + row_index
        rows_a = raw[a]
        if a == 0:
            rows_a = jnp.where(
                row_index == 0, lead[:tile], jnp.where(row_index == 1, lead[tile:], rows_a)
            )
        panel = times_transposed(rows_a, inverse, lax.Precision.HIGHEST)
        update = times_transposed(panel, across, lax.Precision.HIGH)
        parts = []
        for cycle in range(col_cycles):
            col_tile = wanted[cycle]
            value = jittered(slices[cycle][a], cycle, row_tile, col_tile)
            value = value - update[:, cycle * tile : (cycle + 1) * tile]
            if cycle == 0:
                value = jnp.where(col_index == 0, panel[:, :tile], value)
                value = jnp.where(col_index == 1, panel[:, tile:], value)
            keep = row_tile * tile + rows >= col_tile * tile + cols
            parts.append(jnp.where(keep, value, 0.0))
        outs.append(jnp.stack(parts, axis=1))
    return jnp.stack(outs, axis=0)


def solution(mesh):
    in_specs = (P(None, "row", None, "col"), P(None, "col"))
    out_specs = P(None, "row", None, "col")
    return jax.shard_map(body, mesh=mesh, in_specs=in_specs, out_specs=out_specs, check_vma=False)
```
